128 devices in a mesh: lat: 4 (over x_hi, core), lon: 32 (over y, z, x_lo).
Axes of the slice: x: 4 (x_hi: 2, x_lo: 2; x = x_hi * 2 + x_lo), y: 4, z: 4, core: 2. Of those that a mesh axis runs over, the one named last changes fastest.
Arguments:
- starting_vector: bfloat16 [256, 3584, 128], P('lat', 'lon'), may hold values from -6 to 6
- conv_first: bfloat16 [3, 3, 128, 128], replicated, may hold values from -0.1875 to 0.1875
- later_stencil_matrix: bfloat16 [3, 3, 128, 128], replicated, may hold values from -0.1875 to 0.1875
- obs_in: bfloat16 [128, 512], replicated, may hold values from -0.5 to 0.5
- obs_bias: float32 [512], replicated, may hold values from -3 to 3
- obs_out: bfloat16 [512, 256], replicated, may hold values from -0.25 to 0.25
- innovations: bfloat16 [128, 32, 128, 256], P(('lat', 'lon')), may hold values from -6 to 6
- counts: int32 [128, 32], P(('lat', 'lon')), may hold values from 1 to 128, as said below
- columns: int32 [128, 32, 128], P(('lat', 'lon')), may hold values from 0 to 7167
Outputs:
- gradient: float32 [256, 3584, 128], P('lat', 'lon')
The draws below stay inside these ranges and needn't reach their ends.
Inputs may be any that keep to these rules, and one draw needn't show every extreme that they name: `counts`: in every latitude row of devices one longitude tile, drawn, receives 128 live slots from every source of that row.
All inputs are finite; a program needn't handle non-finite values.
Results may differ from the reference program's by a relative error of at most 0.0049.
Values may be sent and summed in bfloat16 or wider, within the bound.
No kernel may reach another device: no remote copies, remote signals or barrier semaphores. Data moves between devices by JAX's collectives and lax.ppermute only.
A program may use at most 128 MiB of HBM per device.

```python
import jax
import jax.numpy as jnp
from jax import lax

C = 128
R = 256
G = 512
HL = 64
WL = 112
CAP = 128
NORTH_SOUTH_SPAN = 256
EAST_WEST_SPAN = 3584
N_LAT = 4
N_LON = 32


def draw_counts(key, part):
    key = jax.random.fold_in(key, 11)
    first, second = jax.random.split(key)
    busy = jax.random.randint(first, (N_LAT,), 0, N_LON)
    base = jax.random.randint(second, (N_LAT, N_LON, N_LON), 1, CAP + 1)
    lon_ids = jnp.arange(N_LON)[None, None, :]
    full = jnp.where(lon_ids == busy[:, None, None], CAP, base)
    return full.reshape(N_LAT * N_LON, N_LON).astype(jnp.int32)


def plant(entries, own_key, low, top_value):
    extent = entries.shape
    spot = [jax.random.randint(jax.random.fold_in(own_key, axis), (), 0, extent[axis]) for axis in range(len(extent))]
    entries = entries.at[tuple(spot)].set(low)
    longest = extent.index(max(extent))
    spot[longest] = (spot[longest] + 1) % extent[longest]
    return entries.at[tuple(spot)].set(top_value)


def block_scale(own_key, shape, shards, low, top_value):
    def one(position, shards_of):
        heights = jax.random.uniform(jax.random.fold_in(jax.random.fold_in(own_key, 6), position), (shards_of,), jnp.float32, low / len(shards), top_value / len(shards))
        return jnp.repeat(jnp.exp(heights), shape[position] // shards_of).reshape((-1,) + (1,) * (len(shape) - position - 1))

    loudness = one(*shards[0])
    for cut in shards[1:]:
        loudness = loudness * one(*cut)
    return loudness


def noise(key, dims, deviation, reach, pieces=(), kind=jnp.bfloat16):
    gain = block_scale(key, dims, pieces, -0.22, 0.18) if pieces else 1.0
    drawn = jax.random.normal(key, dims, jnp.float32) * deviation * gain
    return jnp.minimum(jnp.maximum(drawn, -reach), reach).astype(kind)


def setup_inputs(seed: int = 0) -> dict:
    key_list = jax.random.split(jax.random.key(seed), 10)
    return {
        "starting_vector": noise(key_list[0], (NORTH_SOUTH_SPAN, EAST_WEST_SPAN, C), 1.0, 6.0, ((0, 4), (1, 32))),
        "conv_first": noise(key_list[1], (3, 3, C, C), (9 * C) ** -0.5, 0.1875),
        "later_stencil_matrix": noise(key_list[2], (3, 3, C, C), (9 * C) ** -0.5, 0.1875),
        "obs_in": noise(key_list[3], (C, G), C ** -0.5, 0.5),
        "obs_bias": noise(key_list[4], (G,), 0.5, 3.0, (), jnp.float32),
        "obs_out": noise(key_list[5], (G, R), G ** -0.5, 0.25),
        "innovations": noise(key_list[6], (N_LAT * N_LON, N_LON, CAP, R), 1.0, 6.0, ((0, 128),)),
        "counts": draw_counts(jax.random.fold_in(key_list[9], 71), 0),
        "columns": plant(jax.random.randint(key_list[8], (N_LAT * N_LON, N_LON, CAP), 0, HL * WL), jax.random.fold_in(key_list[8], 1), 0, (HL * WL) - 1).astype(jnp.int32),
    }


def extended_lattice_values(field):
    field = jnp.concatenate([field[:, -1:], field, field[:, :1]], axis=1)
    zero_rows = jnp.zeros((1,) + field.shape[1:], field.dtype)
    return jnp.concatenate([zero_rows, field, zero_rows], axis=0)


def stencil_filter(padded, kernel):
    out_rows = padded.shape[0] - 2
    out_cols = padded.shape[1] - 2
    total = jnp.zeros((out_rows, out_cols, kernel.shape[-1]), jnp.float32)
    for row_off in range(3):
        for col_off in range(3):
            window = padded[row_off:row_off + out_rows, col_off:col_off + out_cols].astype(jnp.float32)
            total = total + jnp.einsum("hwc,cd->hwd", window, kernel[row_off, col_off].astype(jnp.float32))
    return total


def flipped(kernel):
    return jnp.transpose(kernel[::-1, ::-1], (0, 1, 3, 2))


def silu_slope(value):
    sig = jax.nn.sigmoid(value)
    return sig * (1.0 + value * (1.0 - sig))


def observe(patch_extent, radiance_rows, live, obs_in, obs_bias, obs_out):
    z_value = jnp.dot(patch_extent, obs_in, preferred_element_type=jnp.float32) + obs_bias
    u_value = jax.nn.silu(z_value).astype(jnp.bfloat16)
    predicted = jnp.dot(u_value, obs_out, preferred_element_type=jnp.float32)
    misfit = jnp.where(live[:, None], predicted - radiance_rows.astype(jnp.float32), 0.0).astype(jnp.bfloat16)
    back = jnp.dot(misfit, obs_out.T, preferred_element_type=jnp.float32)
    slope = (back * silu_slope(z_value)).astype(jnp.bfloat16)
    return jnp.dot(slope, obs_in.T, preferred_element_type=jnp.float32)


def reference(starting_vector, conv_first, later_stencil_matrix, obs_in, obs_bias, obs_out, innovations, counts, columns):
    pre = stencil_filter(extended_lattice_values(starting_vector), conv_first)
    intermediate_activation = jax.nn.silu(pre).astype(jnp.bfloat16)
    predicted_vector = (starting_vector.astype(jnp.float32) + stencil_filter(extended_lattice_values(intermediate_activation), later_stencil_matrix)).astype(jnp.bfloat16)
    feature_depth = starting_vector.shape[-1]
    linear_prediction = predicted_vector.reshape(NORTH_SOUTH_SPAN * EAST_WEST_SPAN, feature_depth)
    dest_ids = jnp.arange(N_LON, dtype=jnp.int32)[:, None]
    slot_ids = jnp.arange(CAP, dtype=jnp.int32)[None, :]

    def one_source(total, inputs):
        radiance, live_count, cells, source = inputs
        lat_index = source // N_LON
        row_of = lat_index * HL + cells // WL
        col_of = dest_ids * WL + cells % WL
        linear_position = (row_of * EAST_WEST_SPAN + col_of).reshape(-1).astype(jnp.int32)
        live = (slot_ids < live_count[:, None]).reshape(-1)
        patch_extent = linear_prediction[linear_position]
        grads = observe(patch_extent, radiance.reshape(N_LON * CAP, -1), live, obs_in, obs_bias, obs_out)
        return total.at[linear_position].add(grads), None

    sources = jnp.arange(N_LAT * N_LON, dtype=jnp.int32)
    start = jnp.zeros((NORTH_SOUTH_SPAN * EAST_WEST_SPAN, feature_depth), jnp.float32)
    dforecast, _ = lax.scan(one_source, start, (innovations, counts, columns, sources))
    dforecast = dforecast.reshape(NORTH_SOUTH_SPAN, EAST_WEST_SPAN, feature_depth)
    dround = dforecast.astype(jnp.bfloat16)
    dhidden = stencil_filter(extended_lattice_values(dround), flipped(later_stencil_matrix))
    dpre = (dhidden * silu_slope(pre)).astype(jnp.bfloat16)
    return dforecast + stencil_filter(extended_lattice_values(dpre), flipped(conv_first))
```

```python
import jax
import jax.numpy as jnp
from jax import lax
from jax.experimental import pallas as pl
from jax.experimental.pallas import tpu as pltpu
from jax.sharding import PartitionSpec as P

BF = jnp.bfloat16
F32 = jnp.float32
WIDE = 128
PAD = 136
BLOCK = 512
TOTALS = 4


def sigmoid(value):
    return 0.5 * jnp.tanh(0.5 * value) + 0.5


def pair_weights(kernel_ref, out_ref):
    depth = kernel_ref.shape[-1]
    zero = jnp.zeros((depth, depth), BF)
    for row in range(4):
        for col in range(3):
            at = (row * 3 + col) * depth
            out_ref[at : at + depth, :depth] = kernel_ref[row, col] if row < 3 else zero
            out_ref[at : at + depth, depth:] = kernel_ref[row - 1, col] if row > 0 else zero


def taps_across(source_ref, taps_ref, start, width):
    depth = source_ref.shape[-1]
    for col in range(3):
        taps_ref[:, :, :, col * depth : (col + 1) * depth] = source_ref[
            :, :, start + col : start + col + width, :
        ].astype(BF)


def row_pairs(taps_ref, weights_ref, first, last):
    count, width, wide = last - first, taps_ref.shape[2], taps_ref.shape[3]
    rows = [
        taps_ref[first + a // 2 : last + a // 2, a % 2].reshape(count * width, wide)
        for a in range(4)
    ]
    total = jnp.dot(
        jnp.concatenate(rows, axis=1), weights_ref[...], preferred_element_type=F32
    )
    depth = wide // 3
    return (
        total[:, :depth].reshape(count, width, depth),
        total[:, depth:].reshape(count, width, depth),
    )


def spans(total, pieces):
    cuts = [total * i // pieces for i in range(pieces + 1)]
    return list(zip(cuts[:-1], cuts[1:]))


def pad_field(padded_ref, inner, top_ref, bottom_ref, left_ref, right_ref):
    pairs = padded_ref.shape[0]
    width = top_ref.shape[1]
    padded_ref[1 : pairs - 1, :, 8 : 8 + width, :] = inner
    padded_ref[0, :, 8 : 8 + width, :] = top_ref[...].astype(F32)
    padded_ref[pairs - 1, :, 8 : 8 + width, :] = bottom_ref[...].astype(F32)
    padded_ref[:, :, 6:8, :] = left_ref[...].astype(F32).reshape(pairs, 2, 2, -1)
    padded_ref[:, :, 8 + width : 10 + width, :] = right_ref[...].astype(F32).reshape(
        pairs, 2, 2, -1
    )


def forward_kernel(
    edge_ref, x_ref, top_ref, bottom_ref, left_ref, right_ref, first_ref, second_ref,
    forecast_ref, slope_ref,
    padded, taps_one, hidden, taps_two, weights_one, weights_two,
):
    rows, width, depth = x_ref.shape
    pair_weights(first_ref, weights_one)
    pair_weights(second_ref, weights_two)
    pad_field(
        padded, x_ref[...].astype(F32).reshape(rows // 2, 2, width, depth),
        top_ref, bottom_ref, left_ref, right_ref,
    )
    taps_across(padded, taps_one, 6, WIDE)
    pairs = rows // 2 + 1
    for first, last in spans(pairs, 3):
        for odd, pre in enumerate(row_pairs(taps_one, weights_one, first, last)):
            sig = sigmoid(pre)
            hidden[first:last, odd] = pre * sig
            slope_ref[first:last, odd] = sig * (1.0 + pre * (1.0 - sig))
    hidden[0, 0] = hidden[0, 0] * edge_ref[0]
    hidden[pairs - 1, 1] = hidden[pairs - 1, 1] * edge_ref[1]
    taps_across(hidden, taps_two, 0, width)
    for first, last in spans(rows // 2, 4):
        for odd, change in enumerate(row_pairs(taps_two, weights_two, first, last)):
            for pair in range(first, last):
                row = 2 * pair + odd
                forecast_ref[row] = (
                    (x_ref[row].astype(F32) + change[pair - first]).astype(BF).astype(F32)
                )
    forecast_ref[rows] = jnp.zeros((width, depth), F32)


def observe_kernel(
    cells_ref, forecast_ref, into_ref, bias_ref, out_ref, predicted_ref, slope_ref, state
):
    step = pl.program_id(0)

    def take(slot, carry):
        state[pl.ds(slot, 1), :] = forecast_ref[pl.ds(cells_ref[step * BLOCK + slot], 1), :]
        return carry

    lax.fori_loop(0, BLOCK, take, 0, unroll=16)
    z = jnp.dot(state[...].astype(BF), into_ref[...], preferred_element_type=F32) + bias_ref[...]
    sig = sigmoid(z)
    slope_ref[...] = sig * (1.0 + z * (1.0 - sig))
    predicted_ref[...] = jnp.dot(
        (z * sig).astype(BF), out_ref[...], preferred_element_type=F32
    )


def scatter_kernel(
    cells_ref, radiance_ref, predicted_ref, slope_ref, out_t_ref, into_t_ref,
    total_ref, rim_ref, side_ref, grads, *parts,
):
    step = pl.program_id(0)

    @pl.when(step == 0)
    def _():
        for part in parts:
            part[...] = jnp.zeros(part.shape, F32)

    misfit = (predicted_ref[...] - radiance_ref[...].astype(F32)).astype(BF)
    back = jnp.dot(misfit, out_t_ref[...], preferred_element_type=F32)
    grads[...] = jnp.dot(
        (back * slope_ref[...]).astype(BF), into_t_ref[...], preferred_element_type=F32
    )

    def add(group, carry):
        for k, part in enumerate(parts):
            slot = group * len(parts) + k
            at = pl.ds(cells_ref[step * BLOCK + slot], 1)
            part[at, :] = part[at, :] + grads[pl.ds(slot, 1), :]
        return carry

    lax.fori_loop(0, BLOCK // len(parts), add, 0, unroll=4)

    @pl.when(step == pl.num_programs(0) - 1)
    def _():
        rows, width, depth = total_ref.shape
        total = parts[0][: rows * width]
        for part in parts[1:]:
            total = total + part[: rows * width]
        total = total.reshape(rows, width, depth)
        total_ref[...] = total
        rim_ref[0] = total[:2].astype(BF)
        rim_ref[1] = total[rows - 2 :].astype(BF)
        side_ref[0] = total_ref[:, 0:2, :].astype(BF)
        side_ref[1] = total_ref[:, width - 2 : width, :].astype(BF)


def backward_kernel(
    edge_ref, d_ref, top_ref, bottom_ref, left_ref, right_ref, second_ref, first_ref, slope_ref,
    out_ref,
    padded, taps_one, change, taps_two, weights_one, weights_two,
):
    rows, width, depth = d_ref.shape
    pair_weights(second_ref, weights_one)
    pair_weights(first_ref, weights_two)
    pad_field(
        padded, d_ref[...].reshape(rows // 2, 2, width, depth),
        top_ref, bottom_ref, left_ref, right_ref,
    )
    taps_across(padded, taps_one, 6, WIDE)
    pairs = rows // 2 + 1
    for first, last in spans(pairs, 3):
        for odd, dhidden in enumerate(row_pairs(taps_one, weights_one, first, last)):
            change[first:last, odd] = dhidden * slope_ref[first:last, odd]
    change[0, 0] = change[0, 0] * edge_ref[0]
    change[pairs - 1, 1] = change[pairs - 1, 1] * edge_ref[1]
    taps_across(change, taps_two, 0, width)
    for first, last in spans(rows // 2, 4):
        for odd, back in enumerate(row_pairs(taps_two, weights_two, first, last)):
            for pair in range(first, last):
                row = 2 * pair + odd
                out_ref[row] = d_ref[row] + back[pair - first]


VMEM = pl.BlockSpec(memory_space=pltpu.VMEM)
SMEM = pl.BlockSpec(memory_space=pltpu.SMEM)


def params(**more):
    return pltpu.CompilerParams(vmem_limit_bytes=60 * 1024 * 1024, **more)


def conv_scratch(rows, width, depth):
    return [
        pltpu.VMEM((rows // 2 + 2, 2, PAD, depth), F32),
        pltpu.VMEM((rows // 2 + 2, 2, WIDE, 3 * depth), BF),
        pltpu.VMEM((rows // 2 + 1, 2, WIDE, depth), F32),
        pltpu.VMEM((rows // 2 + 1, 2, width, 3 * depth), BF),
        pltpu.VMEM((12 * depth, 2 * depth), BF),
        pltpu.VMEM((12 * depth, 2 * depth), BF),
    ]


def flipped(kernel):
    return jnp.transpose(kernel[::-1, ::-1], (0, 1, 3, 2))


def shifted(array, axis, step, wrap):
    count = lax.axis_size(axis)
    return lax.ppermute(
        array, axis, [(i, (i + step) % count) for i in range(count) if wrap or 0 <= i + step < count]
    )


def border(head, tail, left, right):
    top = shifted(tail, "lat", 1, False)
    bottom = shifted(head, "lat", -1, False)
    left = jnp.concatenate([top[:, :2], left, bottom[:, :2]], axis=0)
    right = jnp.concatenate([top[:, -2:], right, bottom[:, -2:]], axis=0)
    return top, bottom, shifted(right, "lon", 1, True), shifted(left, "lon", -1, True)


def per_device(
    starting_vector, conv_first, later_stencil_matrix, obs_in, obs_bias, obs_out,
    innovations, counts, columns,
):
    rows, width, depth = starting_vector.shape
    lon_count, slots, channels = innovations.shape[1:]
    hidden_units = obs_in.shape[1]
    taken = lon_count * slots
    lat = lax.axis_index("lat")
    edge = jnp.stack([lat > 0, lat < lax.axis_size("lat") - 1]).astype(F32)

    live = lax.iota(jnp.int32, slots)[None, :] < counts[0][:, None]
    cells = jnp.where(live, columns[0], rows * width)
    cells = lax.all_to_all(cells, "lon", 0, 0, tiled=True).reshape(-1)
    radiance = lax.all_to_all(innovations[0], "lon", 0, 0, tiled=True).reshape(taken, channels)

    x = starting_vector
    ring = border(x[:2], x[-2:], x[:, :2], x[:, -2:])
    pairs = rows // 2 + 1
    forecast, slope = pl.pallas_call(
        forward_kernel,
        out_shape=(
            jax.ShapeDtypeStruct((rows + 1, width, depth), F32),
            jax.ShapeDtypeStruct((pairs, 2, WIDE, depth), F32),
        ),
        in_specs=[SMEM] + [VMEM] * 7,
        out_specs=(VMEM, VMEM),
        scratch_shapes=conv_scratch(rows, width, depth),
        compiler_params=params(),
        name="forward",
    )(edge, x, *ring, conv_first, later_stencil_matrix)

    predicted, z_slope = pl.pallas_call(
        observe_kernel,
        grid=(taken // BLOCK,),
        out_shape=(
            jax.ShapeDtypeStruct((taken, channels), F32),
            jax.ShapeDtypeStruct((taken, hidden_units), F32),
        ),
        in_specs=[SMEM] + [VMEM] * 4,
        out_specs=(
            pl.BlockSpec((BLOCK, channels), lambda i: (i, 0)),
            pl.BlockSpec((BLOCK, hidden_units), lambda i: (i, 0)),
        ),
        scratch_shapes=[pltpu.VMEM((BLOCK, depth), F32)],
        compiler_params=params(),
        name="observe",
    )(cells, forecast.reshape((rows + 1) * width, depth), obs_in, obs_bias[None], obs_out)

    dforecast, rim, side = pl.pallas_call(
        scatter_kernel,
        grid=(taken // BLOCK,),
        out_shape=(
            jax.ShapeDtypeStruct((rows, width, depth), F32),
            jax.ShapeDtypeStruct((2, 2, width, depth), BF),
            jax.ShapeDtypeStruct((2, rows, 2, depth), BF),
        ),
        in_specs=[
            SMEM,
            pl.BlockSpec((BLOCK, channels), lambda i: (i, 0)),
            pl.BlockSpec((BLOCK, channels), lambda i: (i, 0)),
            pl.BlockSpec((BLOCK, hidden_units), lambda i: (i, 0)),
            VMEM,
            VMEM,
        ],
        out_specs=(VMEM, VMEM, VMEM),
        scratch_shapes=[pltpu.VMEM((BLOCK, depth), F32)]
        + [pltpu.VMEM((rows * width + 8, depth), F32)] * TOTALS,
        compiler_params=params(),
        name="scatter",
    )(cells, radiance, predicted, z_slope, obs_out.T, obs_in.T)

    ring = border(rim[0], rim[1], side[0], side[1])
    return pl.pallas_call(
        backward_kernel,
        out_shape=jax.ShapeDtypeStruct((rows, width, depth), F32),
        in_specs=[SMEM] + [VMEM] * 8,
        out_specs=VMEM,
        scratch_shapes=conv_scratch(rows, width, depth),
        compiler_params=params(),
        name="backward",
    )(edge, dforecast, *ring, flipped(later_stencil_matrix), flipped(conv_first), slope)


def solution(mesh):
    placed = (
        P("lat", "lon", None),
        P(),
        P(),
        P(),
        P(),
        P(),
        P(("lat", "lon"), None, None, None),
        P(("lat", "lon"), None),
        P(("lat", "lon"), None, None),
    )
    return jax.shard_map(
        per_device, mesh=mesh, in_specs=placed, out_specs=P("lat", "lon", None), check_vma=False
    )
```

```python
import jax
import jax.numpy as jnp
from jax import lax
from jax.experimental import pallas as pl
from jax.experimental.pallas import tpu as pltpu
from jax.sharding import PartitionSpec as P

BF = jnp.bfloat16
F32 = jnp.float32
WIDE = 128
PAD = 136
BLOCK = 512
TOTALS = 4


def sigmoid(value):
    return 0.5 * jnp.tanh(0.5 * value) + 0.5


def pair_weights(kernel_ref, out_ref):
    depth = kernel_ref.shape[-1]
    zero = jnp.zeros((depth, depth), BF)
    for row in range(4):
        for col in range(3):
            at = (row * 3 + col) * depth
            out_ref[at : at + depth, :depth] = kernel_ref[row, col] if row < 3 else zero
            out_ref[at : at + depth, depth:] = kernel_ref[row - 1, col] if row > 0 else zero


def flipped_weights(kernel_ref, out_ref):
    depth = kernel_ref.shape[-1]
    zero = jnp.zeros((depth, depth), BF)
    for row in range(4):
        for col in range(3):
            at = (row * 3 + col) * depth
            out_ref[at : at + depth, :depth] = kernel_ref[2 - row, 2 - col].T if row < 3 else zero
            out_ref[at : at + depth, depth:] = kernel_ref[3 - row, 2 - col].T if row > 0 else zero


def clear_outside(ring):
    lat = lax.axis_index("lat")
    last = ring.shape[0] - 1
    ring[0, 0] = jnp.where(lat > 0, ring[0, 0], 0.0)
    ring[last, 1] = jnp.where(lat < lax.axis_size("lat") - 1, ring[last, 1], 0.0)


def taps_across(source_ref, taps_ref, start, width):
    depth = source_ref.shape[-1]
    for col in range(3):
        taps_ref[:, :, :, col * depth : (col + 1) * depth] = source_ref[
            :, :, start + col : start + col + width, :
        ].astype(BF)


def row_pairs(taps_ref, weights_ref, first, last):
    count, width, wide = last - first, taps_ref.shape[2], taps_ref.shape[3]
    rows = [
        taps_ref[first + a // 2 : last + a // 2, a % 2].reshape(count * width, wide)
        for a in range(4)
    ]
    total = jnp.dot(
        jnp.concatenate(rows, axis=1), weights_ref[...], preferred_element_type=F32
    )
    depth = wide // 3
    return (
        total[:, :depth].reshape(count, width, depth),
        total[:, depth:].reshape(count, width, depth),
    )


def spans(total, pieces):
    cuts = [total * i // pieces for i in range(pieces + 1)]
    return list(zip(cuts[:-1], cuts[1:]))


def pad_rim(padded_ref, top_ref, bottom_ref, left_ref, right_ref):
    pairs = padded_ref.shape[0]
    width = top_ref.shape[1]
    padded_ref[0, :, 8 : 8 + width, :] = top_ref[...].astype(F32)
    padded_ref[pairs - 1, :, 8 : 8 + width, :] = bottom_ref[...].astype(F32)
    padded_ref[:, :, 6:8, :] = left_ref[...].astype(F32).reshape(pairs, 2, 2, -1)
    padded_ref[:, :, 8 + width : 10 + width, :] = right_ref[...].astype(F32).reshape(
        pairs, 2, 2, -1
    )


def forward_kernel(
    cells_ref, top_ref, bottom_ref, left_ref, right_ref, bias_ref,
    x_hbm, first_hbm, second_hbm, into_hbm, out_hbm,
    predicted_hbm, z_slope_hbm, slope_hbm, second_back_hbm, first_back_hbm,
    padded, taps_one, hidden, taps_two, weights_one, weights_two, forecast, state,
    x_ref, first_ref, second_ref, into_ref, out_ref, sems,
    predicted_ref, z_slope_ref, slope_ref, second_back_ref, first_back_ref, out_sems,
):
    leaving = []

    def leave(source, into):
        leaving.append(pltpu.make_async_copy(source, into, out_sems.at[len(leaving)]))
        leaving[-1].start()

    sources = (x_hbm, first_hbm, second_hbm, into_hbm, out_hbm)
    fetched = (x_ref, first_ref, second_ref, into_ref, out_ref)
    copies = [
        pltpu.make_async_copy(source, into, sems.at[k])
        for k, (source, into) in enumerate(zip(sources, fetched))
    ]
    for copy in copies:
        copy.start()
    rows, width, depth = x_ref.shape
    for copy in copies:
        copy.wait()
    pair_weights(first_ref, weights_one)
    pair_weights(second_ref, weights_two)
    padded[1 : rows // 2 + 1, :, 8 : 8 + width, :] = (
        x_ref[...].astype(F32).reshape(rows // 2, 2, width, depth)
    )
    pad_rim(padded, top_ref, bottom_ref, left_ref, right_ref)
    taps_across(padded, taps_one, 6, WIDE)
    pairs = rows // 2 + 1
    for first, last in spans(pairs, 3):
        for odd, pre in enumerate(row_pairs(taps_one, weights_one, first, last)):
            sig = sigmoid(pre)
            hidden[first:last, odd] = pre * sig
            slope_ref[first:last, odd] = sig * (1.0 + pre * (1.0 - sig))
    leave(slope_ref, slope_hbm)
    clear_outside(hidden)
    taps_across(hidden, taps_two, 0, width)
    for first, last in spans(rows // 2, 4):
        for odd, change in enumerate(row_pairs(taps_two, weights_two, first, last)):
            for pair in range(first, last):
                row = 2 * pair + odd
                forecast[row * width : (row + 1) * width] = (
                    (x_ref[row].astype(F32) + change[pair - first]).astype(BF).astype(F32)
                )
    forecast[rows * width :] = jnp.zeros((forecast.shape[0] - rows * width, depth), F32)
    flipped_weights(second_ref, second_back_ref)
    flipped_weights(first_ref, first_back_ref)
    leave(second_back_ref, second_back_hbm)
    leave(first_back_ref, first_back_hbm)

    def take(slot, carry):
        state[pl.ds(slot, 1), :] = forecast[pl.ds(cells_ref[slot], 1), :]
        return carry

    taken = state.shape[0]
    lax.fori_loop(0, taken, take, 0, unroll=64)
    for first in range(0, taken, BLOCK):
        at = slice(first, first + BLOCK)
        z = jnp.dot(state[at].astype(BF), into_ref[...], preferred_element_type=F32)
        z = z + bias_ref[...]
        sig = sigmoid(z)
        z_slope_ref[at] = (sig * (1.0 + z * (1.0 - sig))).astype(BF)
        predicted_ref[at] = jnp.dot(
            (z * sig).astype(BF), out_ref[...], preferred_element_type=F32
        )
        leave(predicted_ref.at[at], predicted_hbm.at[at])
        leave(z_slope_ref.at[at], z_slope_hbm.at[at])
    for copy in leaving:
        copy.wait()


def scatter_kernel(
    cells_ref, out_t_ref, into_t_ref, radiance_hbm, predicted_hbm, z_slope_hbm,
    total_ref, head_ref, tail_ref, left_ref, right_ref,
    radiance, predicted, z_slope, sems, grads, *parts,
):
    taken = grads.shape[0]
    blocks = [slice(first, first + BLOCK) for first in range(0, taken, BLOCK)]
    copies = [
        [
            pltpu.make_async_copy(source.at[at], into.at[at], sems.at[k, j])
            for j, (source, into) in enumerate(
                ((radiance_hbm, radiance), (predicted_hbm, predicted), (z_slope_hbm, z_slope))
            )
        ]
        for k, at in enumerate(blocks)
    ]
    for group in copies:
        for copy in group:
            copy.start()
    for part in parts:
        part[...] = jnp.zeros(part.shape, F32)
    for at, group in zip(blocks, copies):
        for copy in group:
            copy.wait()
        misfit = (predicted[at] - radiance[at].astype(F32)).astype(BF)
        back = jnp.dot(misfit, out_t_ref[...], preferred_element_type=F32)
        grads[at] = jnp.dot(
            (back * z_slope[at].astype(F32)).astype(BF), into_t_ref[...], preferred_element_type=F32
        )

    def add(group, carry):
        slots = [group * len(parts) + k for k in range(len(parts))]
        ats = [pl.ds(cells_ref[slot], 1) for slot in slots]
        sums = [
            part[at, :] + grads[pl.ds(slot, 1), :] for part, at, slot in zip(parts, ats, slots)
        ]
        for part, at, value in zip(parts, ats, sums):
            part[at, :] = value
        return carry

    lax.fori_loop(0, taken // len(parts), add, 0, unroll=8)
    rows, width, depth = total_ref.shape
    total = parts[0][: rows * width]
    for part in parts[1:]:
        total = total + part[: rows * width]
    total = total.reshape(rows, width, depth)
    total_ref[...] = total
    head_ref[...] = total[:2].astype(BF)
    tail_ref[...] = total[rows - 2 :].astype(BF)
    left_ref[...] = total_ref[:, 0:2, :].astype(BF)
    right_ref[...] = total_ref[:, width - 2 : width, :].astype(BF)


def backward_kernel(
    d_ref, top_ref, bottom_ref, left_ref, right_ref, weights_one, weights_two, slope_ref,
    out_hbm,
    padded, taps_one, change, taps_two, out, sems,
):
    rows, width, depth = out.shape
    pairs = rows // 2 + 1
    padded[1:pairs, :, 8 : 8 + width] = d_ref[...].reshape(rows // 2, 2, width, depth)
    pad_rim(padded, top_ref, bottom_ref, left_ref, right_ref)
    taps_across(padded, taps_one, 6, WIDE)
    for first, last in spans(pairs, 3):
        for odd, dhidden in enumerate(row_pairs(taps_one, weights_one, first, last)):
            change[first:last, odd] = dhidden * slope_ref[first:last, odd]
    clear_outside(change)
    taps_across(change, taps_two, 0, width)
    leaving = []
    for k, (first, last) in enumerate(spans(rows // 2, 4)):
        for odd, back in enumerate(row_pairs(taps_two, weights_two, first, last)):
            for pair in range(first, last):
                out[2 * pair + odd] = d_ref[2 * pair + odd] + back[pair - first]
        at = slice(2 * first, 2 * last)
        leaving.append(pltpu.make_async_copy(out.at[at], out_hbm.at[at], sems.at[k]))
        leaving[-1].start()
    for copy in leaving:
        copy.wait()


VMEM = pl.BlockSpec(memory_space=pltpu.VMEM)
SMEM = pl.BlockSpec(memory_space=pltpu.SMEM)
HBM = pl.BlockSpec(memory_space=pltpu.HBM)


def params(mebibytes):
    return pltpu.CompilerParams(vmem_limit_bytes=mebibytes * 1024 * 1024)


def conv_scratch(rows, width, depth):
    return [
        pltpu.VMEM((rows // 2 + 2, 2, PAD, depth), F32),
        pltpu.VMEM((rows // 2 + 2, 2, WIDE, 3 * depth), BF),
        pltpu.VMEM((rows // 2 + 1, 2, WIDE, depth), F32),
        pltpu.VMEM((rows // 2 + 1, 2, width, 3 * depth), BF),
    ]


def swapped(array, axis, first, around):
    count = lax.axis_size(axis)
    pairs = [(i, (i + 1) % count) for i in range(first, count, 2) if around or i + 1 < count]
    return lax.ppermute(array, axis, [way for i, j in pairs for way in ((i, j), (j, i))])


def neighbours(low, high, axis, around):
    even = lax.rem(lax.axis_index(axis), 2) == 0
    one = swapped(jnp.where(even, high, low), axis, 0, around)
    two = swapped(jnp.where(even, low, high), axis, 1, around)
    return jnp.where(even, two, one), jnp.where(even, one, two)


def rows_around(head, tail):
    return neighbours(head, tail, "lat", False)


def columns_around(top, bottom, left, right):
    left = jnp.concatenate([top[:, :2], left, bottom[:, :2]], axis=0)
    right = jnp.concatenate([top[:, -2:], right, bottom[:, -2:]], axis=0)
    return neighbours(left, right, "lon", True)


def per_device(
    starting_vector, conv_first, later_stencil_matrix, obs_in, obs_bias, obs_out,
    innovations, counts, columns,
):
    rows, width, depth = starting_vector.shape
    lon_count, slots, channels = innovations.shape[1:]
    hidden_units = obs_in.shape[1]
    taken = lon_count * slots
    pairs = rows // 2 + 1

    live = lax.iota(jnp.int32, slots)[None, :] < counts[0][:, None]
    cells = jnp.where(live, columns[0], rows * width)
    cells = lax.all_to_all(cells, "lon", 0, 0, tiled=True).reshape(-1)
    x = starting_vector
    top, bottom = rows_around(x[:2], x[-2:])
    top, bottom, cells = lax.optimization_barrier((top, bottom, cells))
    ring = (top, bottom, *columns_around(top, bottom, x[:, :2], x[:, -2:]))
    ring, radiance = lax.optimization_barrier((ring, innovations[0]))
    radiance = lax.all_to_all(radiance, "lon", 0, 0, tiled=True).reshape(taken, channels)

    weights = jax.ShapeDtypeStruct((12 * depth, 2 * depth), BF)
    fetched = (x, conv_first, later_stencil_matrix, obs_in, obs_out)
    predicted, z_slope, slope, second_back, first_back = pl.pallas_call(
        forward_kernel,
        out_shape=(
            jax.ShapeDtypeStruct((taken, channels), F32),
            jax.ShapeDtypeStruct((taken, hidden_units), BF),
            jax.ShapeDtypeStruct((pairs, 2, WIDE, depth), F32),
            weights,
            weights,
        ),
        in_specs=[SMEM] + [VMEM] * 5 + [HBM] * 5,
        out_specs=(HBM,) * 5,
        scratch_shapes=conv_scratch(rows, width, depth)
        + [pltpu.VMEM((12 * depth, 2 * depth), BF)] * 2
        + [pltpu.VMEM((rows * width + 8, depth), F32), pltpu.VMEM((taken, depth), F32)]
        + [pltpu.VMEM(array.shape, array.dtype) for array in fetched]
        + [pltpu.SemaphoreType.DMA((len(fetched),))]
        + [
            pltpu.VMEM((taken, channels), F32),
            pltpu.VMEM((taken, hidden_units), BF),
            pltpu.VMEM((pairs, 2, WIDE, depth), F32),
            pltpu.VMEM(weights.shape, BF),
            pltpu.VMEM(weights.shape, BF),
            pltpu.SemaphoreType.DMA((3 + 2 * taken // BLOCK,)),
        ],
        compiler_params=params(60),
        name="forward",
    )(cells, *ring, obs_bias[None], *fetched)

    side = jax.ShapeDtypeStruct((rows, 2, depth), BF)
    edge = jax.ShapeDtypeStruct((2, width, depth), BF)
    dforecast, head, tail, left, right = pl.pallas_call(
        scatter_kernel,
        out_shape=(jax.ShapeDtypeStruct((rows, width, depth), F32), edge, edge, side, side),
        in_specs=[SMEM] + [VMEM] * 2 + [HBM] * 3,
        out_specs=(VMEM,) * 5,
        scratch_shapes=[
            pltpu.VMEM((taken, channels), BF),
            pltpu.VMEM((taken, channels), F32),
            pltpu.VMEM((taken, hidden_units), BF),
            pltpu.SemaphoreType.DMA((taken // BLOCK, 3)),
            pltpu.VMEM((taken, depth), F32),
        ]
        + [pltpu.VMEM((rows * width + 8, depth), F32)] * TOTALS,
        compiler_params=params(45),
        name="scatter",
    )(cells, obs_out.T, obs_in.T, radiance, predicted, z_slope)

    top, bottom = rows_around(head, tail)
    ring = (top, bottom, *columns_around(top, bottom, left, right))
    return pl.pallas_call(
        backward_kernel,
        out_shape=jax.ShapeDtypeStruct((rows, width, depth), F32),
        in_specs=[VMEM] * 8,
        out_specs=HBM,
        scratch_shapes=conv_scratch(rows, width, depth)
        + [pltpu.VMEM((rows, width, depth), F32), pltpu.SemaphoreType.DMA((4,))],
        compiler_params=params(34),
        name="backward",
    )(dforecast, *ring, second_back, first_back, slope)


def solution(mesh):
    placed = (
        P("lat", "lon", None),
        P(),
        P(),
        P(),
        P(),
        P(),
        P(("lat", "lon"), None, None, None),
        P(("lat", "lon"), None),
        P(("lat", "lon"), None, None),
    )
    return jax.shard_map(
        per_device, mesh=mesh, in_specs=placed, out_specs=P("lat", "lon", None), check_vma=False
    )
```

```python
import jax
import jax.numpy as jnp
from jax import lax
from jax.experimental import pallas as pl
from jax.experimental.pallas import tpu as pltpu
from jax.sharding import PartitionSpec as P

BF = jnp.bfloat16
F32 = jnp.float32
WIDE = 128
PAD = 136
BLOCK = 512
GROUP = 1024
TOTALS = 4


def sigmoid(value):
    return 0.5 * jnp.tanh(0.5 * value) + 0.5


def pair_weights(kernel_ref, out_ref):
    depth = kernel_ref.shape[-1]
    zero = jnp.zeros((depth, depth), BF)
    for row in range(4):
        for col in range(3):
            at = (row * 3 + col) * depth
            out_ref[at : at + depth, :depth] = kernel_ref[row, col] if row < 3 else zero
            out_ref[at : at + depth, depth:] = kernel_ref[row - 1, col] if row > 0 else zero


def flipped_weights(kernel_ref, out_ref):
    depth = kernel_ref.shape[-1]
    zero = jnp.zeros((depth, depth), BF)
    for row in range(4):
        for col in range(3):
            at = (row * 3 + col) * depth
            out_ref[at : at + depth, :depth] = kernel_ref[2 - row, 2 - col].T if row < 3 else zero
            out_ref[at : at + depth, depth:] = kernel_ref[3 - row, 2 - col].T if row > 0 else zero


def clear_outside(ring):
    lat = lax.axis_index("lat")
    last = ring.shape[0] - 1
    ring[0, 0] = jnp.where(lat > 0, ring[0, 0], 0.0)
    ring[last, 1] = jnp.where(lat < lax.axis_size("lat") - 1, ring[last, 1], 0.0)


def taps_across(source_ref, taps_ref, start, width, first=0, last=None):
    depth = source_ref.shape[-1]
    of = slice(first, source_ref.shape[0] if last is None else last)
    for col in range(3):
        taps_ref[of, :, :, col * depth : (col + 1) * depth] = source_ref[
            of, :, start + col : start + col + width, :
        ].astype(BF)


def row_pairs(taps_ref, weights_ref, first, last):
    count, width, wide = last - first, taps_ref.shape[2], taps_ref.shape[3]
    rows = [
        taps_ref[first + a // 2 : last + a // 2, a % 2].reshape(count * width, wide)
        for a in range(4)
    ]
    total = jnp.dot(
        jnp.concatenate(rows, axis=1), weights_ref[...], preferred_element_type=F32
    )
    depth = wide // 3
    return (
        total[:, :depth].reshape(count, width, depth),
        total[:, depth:].reshape(count, width, depth),
    )


def spans(total, pieces):
    cuts = [total * i // pieces for i in range(pieces + 1)]
    return list(zip(cuts[:-1], cuts[1:]))


def pad_rim(padded_ref, top_ref, bottom_ref, left_ref, right_ref):
    pairs = padded_ref.shape[0]
    width = top_ref.shape[1]
    padded_ref[0, :, 8 : 8 + width, :] = top_ref[...].astype(F32)
    padded_ref[pairs - 1, :, 8 : 8 + width, :] = bottom_ref[...].astype(F32)
    padded_ref[:, :, 6:8, :] = left_ref[...].astype(F32).reshape(pairs, 2, 2, -1)
    padded_ref[:, :, 8 + width : 10 + width, :] = right_ref[...].astype(F32).reshape(
        pairs, 2, 2, -1
    )


def forward_kernel(
    cells_ref, top_ref, bottom_ref, left_ref, right_ref, bias_ref,
    x_hbm, first_hbm, second_hbm, into_hbm, out_hbm,
    predicted_hbm, z_slope_hbm, slope_hbm, second_back_hbm, first_back_hbm, cells_hbm,
    padded, taps_one, hidden, taps_two, weights_one, weights_two, forecast, state,
    x_ref, first_ref, second_ref, into_ref, out_ref, sems,
    predicted_ref, z_slope_ref, slope_ref, second_back_ref, first_back_ref, out_sems,
):
    leaving = []

    def leave(source, into):
        leaving.append(pltpu.make_async_copy(source, into, out_sems.at[len(leaving)]))
        leaving[-1].start()

    sources = (x_hbm, first_hbm, second_hbm, into_hbm, out_hbm)
    fetched = (x_ref, first_ref, second_ref, into_ref, out_ref)
    copies = [
        pltpu.make_async_copy(source, into, sems.at[k])
        for k, (source, into) in enumerate(zip(sources, fetched))
    ]
    for copy in copies:
        copy.start()
    rows, width, depth = x_ref.shape
    for copy in copies:
        copy.wait()
    pair_weights(first_ref, weights_one)
    pair_weights(second_ref, weights_two)
    padded[1 : rows // 2 + 1, :, 8 : 8 + width, :] = (
        x_ref[...].astype(F32).reshape(rows // 2, 2, width, depth)
    )
    pad_rim(padded, top_ref, bottom_ref, left_ref, right_ref)
    taps_across(padded, taps_one, 6, WIDE)
    pairs = rows // 2 + 1
    for first, last in spans(pairs, 3):
        for odd, pre in enumerate(row_pairs(taps_one, weights_one, first, last)):
            sig = sigmoid(pre)
            hidden[first:last, odd] = pre * sig
            slope_ref[first:last, odd] = sig * (1.0 + pre * (1.0 - sig))
    leave(slope_ref, slope_hbm)
    clear_outside(hidden)
    taps_across(hidden, taps_two, 0, width)
    for first, last in spans(rows // 2, 4):
        for odd, change in enumerate(row_pairs(taps_two, weights_two, first, last)):
            for pair in range(first, last):
                row = 2 * pair + odd
                forecast[row * width : (row + 1) * width] = (
                    (x_ref[row].astype(F32) + change[pair - first]).astype(BF).astype(F32)
                )
    forecast[rows * width :] = jnp.zeros((forecast.shape[0] - rows * width, depth), F32)
    flipped_weights(second_ref, second_back_ref)
    flipped_weights(first_ref, first_back_ref)
    leave(cells_ref, cells_hbm.at[pl.ds(0, cells_ref.shape[0])])
    leave(second_back_ref, second_back_hbm)
    leave(first_back_ref, first_back_hbm)

    def take(slot, carry):
        state[pl.ds(slot, 1), :] = forecast[pl.ds(cells_ref[slot], 1), :]
        return carry

    taken = state.shape[0]
    lax.fori_loop(0, taken, take, 0, unroll=64)
    for first in range(0, taken, BLOCK):
        at = slice(first, first + BLOCK)
        z = jnp.dot(state[at].astype(BF), into_ref[...], preferred_element_type=F32)
        z = z + bias_ref[...]
        sig = sigmoid(z)
        z_slope_ref[at] = (sig * (1.0 + z * (1.0 - sig))).astype(BF)
        predicted_ref[at] = jnp.dot(
            (z * sig).astype(BF), out_ref[...], preferred_element_type=F32
        )
        leave(predicted_ref.at[at], predicted_hbm.at[at])
        leave(z_slope_ref.at[at], z_slope_hbm.at[at])
    for copy in leaving:
        copy.wait()


def scatter_kernel(
    out_t_ref, into_t_ref, radiance_ref, predicted_hbm, z_slope_hbm, cells_hbm,
    total_ref, head_ref, tail_ref, left_ref, right_ref,
    predicted, z_slope, sems, cells_ref, cells_sem, grads, *parts,
):
    taken = grads.shape[0]
    cells_copy = pltpu.make_async_copy(cells_hbm.at[pl.ds(0, taken)], cells_ref, cells_sem)
    cells_copy.start()
    blocks = [slice(first, first + GROUP) for first in range(0, taken, GROUP)]
    copies = [
        [
            pltpu.make_async_copy(source.at[at], into.at[at], sems.at[k, j])
            for j, (source, into) in enumerate(
                ((predicted_hbm, predicted), (z_slope_hbm, z_slope))
            )
        ]
        for k, at in enumerate(blocks)
    ]
    for group in copies:
        for copy in group:
            copy.start()
    for part in parts:
        part[...] = jnp.zeros(part.shape, F32)
    cells_copy.wait()

    def add(group, carry):
        slots = [group * len(parts) + k for k in range(len(parts))]
        ats = [pl.ds(cells_ref[slot], 1) for slot in slots]
        sums = [
            part[at, :] + grads[pl.ds(slot, 1), :] for part, at, slot in zip(parts, ats, slots)
        ]
        for part, at, value in zip(parts, ats, sums):
            part[at, :] = value
        return carry

    for at, group in zip(blocks, copies):
        for copy in group:
            copy.wait()
        misfit = (predicted[at] - radiance_ref[at].astype(F32)).astype(BF)
        back = jnp.dot(misfit, out_t_ref[...], preferred_element_type=F32)
        grads[at] = jnp.dot(
            (back * z_slope[at].astype(F32)).astype(BF),
            into_t_ref[...],
            preferred_element_type=F32,
        )
        lax.fori_loop(at.start // len(parts), at.stop // len(parts), add, 0, unroll=8)
    rows, width, depth = total_ref.shape
    total = parts[0][: rows * width]
    for part in parts[1:]:
        total = total + part[: rows * width]
    total = total.reshape(rows, width, depth)
    total_ref[...] = total
    head_ref[...] = total[:2].astype(BF)
    tail_ref[...] = total[rows - 2 :].astype(BF)
    left_ref[...] = total_ref[:, 0:2, :].astype(BF)
    right_ref[...] = total_ref[:, width - 2 : width, :].astype(BF)


def backward_kernel(
    d_ref, top_ref, bottom_ref, left_ref, right_ref, weights_one, weights_two, slope_ref,
    out_hbm,
    padded, taps_one, change, taps_two, out, sems,
):
    rows, width, depth = out.shape
    pairs = rows // 2 + 1
    pad_rim(padded, top_ref, bottom_ref, left_ref, right_ref)
    made = 0
    for first, last in spans(pairs, 6):
        low, high = max(made, 1), min(last + 1, pairs)
        padded[low:high, :, 8 : 8 + width] = d_ref[2 * low - 2 : 2 * high - 2].reshape(
            high - low, 2, width, depth
        )
        taps_across(padded, taps_one, 6, WIDE, made, last + 1)
        made = last + 1
        for odd, dhidden in enumerate(row_pairs(taps_one, weights_one, first, last)):
            change[first:last, odd] = dhidden * slope_ref[first:last, odd]
    clear_outside(change)
    made = 0
    leaving = []
    for k, (first, last) in enumerate(spans(rows // 2, 8)):
        taps_across(change, taps_two, 0, width, made, last + 1)
        made = last + 1
        for odd, back in enumerate(row_pairs(taps_two, weights_two, first, last)):
            for pair in range(first, last):
                out[2 * pair + odd] = d_ref[2 * pair + odd] + back[pair - first]
        at = slice(2 * first, 2 * last)
        leaving.append(pltpu.make_async_copy(out.at[at], out_hbm.at[at], sems.at[k]))
        leaving[-1].start()
    for copy in leaving:
        copy.wait()


VMEM = pl.BlockSpec(memory_space=pltpu.VMEM)
SMEM = pl.BlockSpec(memory_space=pltpu.SMEM)
HBM = pl.BlockSpec(memory_space=pltpu.HBM)


def params(mebibytes):
    return pltpu.CompilerParams(vmem_limit_bytes=mebibytes * 1024 * 1024)


def conv_scratch(rows, width, depth):
    return [
        pltpu.VMEM((rows // 2 + 2, 2, PAD, depth), F32),
        pltpu.VMEM((rows // 2 + 2, 2, WIDE, 3 * depth), BF),
        pltpu.VMEM((rows // 2 + 1, 2, WIDE, depth), F32),
        pltpu.VMEM((rows // 2 + 1, 2, width, 3 * depth), BF),
    ]


def swapped(array, axis, first, around):
    count = lax.axis_size(axis)
    pairs = [(i, (i + 1) % count) for i in range(first, count, 2) if around or i + 1 < count]
    return lax.ppermute(array, axis, [way for i, j in pairs for way in ((i, j), (j, i))])


def neighbours(low, high, axis, around, after=()):
    even = lax.rem(lax.axis_index(axis), 2) == 0
    one = swapped(jnp.where(even, high, low), axis, 0, around)
    two = swapped(jnp.where(even, low, high), axis, 1, around)
    one, two, after = lax.optimization_barrier((one, two, after))
    return (jnp.where(even, two, one), jnp.where(even, one, two)), after


def rows_around(head, tail):
    return neighbours(head, tail, "lat", False)[0]


def columns_around(top, bottom, left, right, after=()):
    left = jnp.concatenate([top[:, :2], left, bottom[:, :2]], axis=0)
    right = jnp.concatenate([top[:, -2:], right, bottom[:, -2:]], axis=0)
    return neighbours(left, right, "lon", True, after)


def per_device(
    starting_vector, conv_first, later_stencil_matrix, obs_in, obs_bias, obs_out,
    innovations, counts, columns,
):
    rows, width, depth = starting_vector.shape
    lon_count, slots, channels = innovations.shape[1:]
    hidden_units = obs_in.shape[1]
    taken = lon_count * slots
    pairs = rows // 2 + 1

    live = lax.iota(jnp.int32, slots)[None, :] < counts[0][:, None]
    cells = jnp.where(live, columns[0], rows * width)
    cells = lax.all_to_all(cells, "lon", 0, 0, tiled=True).reshape(-1)
    x = starting_vector
    top, bottom = rows_around(x[:2], x[-2:])
    top, bottom, cells = lax.optimization_barrier((top, bottom, cells))
    sides, radiance = columns_around(top, bottom, x[:, :2], x[:, -2:], innovations[0])
    ring = (top, bottom, *sides)
    radiance = lax.all_to_all(radiance, "lon", 0, 0, tiled=True).reshape(taken, channels)

    weights = jax.ShapeDtypeStruct((12 * depth, 2 * depth), BF)
    fetched = (x, conv_first, later_stencil_matrix, obs_in, obs_out)
    predicted, z_slope, slope, second_back, first_back, cells = pl.pallas_call(
        forward_kernel,
        out_shape=(
            jax.ShapeDtypeStruct((taken, channels), F32),
            jax.ShapeDtypeStruct((taken, hidden_units), BF),
            jax.ShapeDtypeStruct((pairs, 2, WIDE, depth), F32),
            weights,
            weights,
            jax.ShapeDtypeStruct((taken * 1024,), jnp.int32),
        ),
        in_specs=[SMEM] + [VMEM] * 5 + [HBM] * 5,
        out_specs=(HBM,) * 6,
        scratch_shapes=conv_scratch(rows, width, depth)
        + [pltpu.VMEM((12 * depth, 2 * depth), BF)] * 2
        + [pltpu.VMEM((rows * width + 8, depth), F32), pltpu.VMEM((taken, depth), F32)]
        + [pltpu.VMEM(array.shape, array.dtype) for array in fetched]
        + [pltpu.SemaphoreType.DMA((len(fetched),))]
        + [
            pltpu.VMEM((taken, channels), F32),
            pltpu.VMEM((taken, hidden_units), BF),
            pltpu.VMEM((pairs, 2, WIDE, depth), F32),
            pltpu.VMEM(weights.shape, BF),
            pltpu.VMEM(weights.shape, BF),
            pltpu.SemaphoreType.DMA((4 + 2 * taken // BLOCK,)),
        ],
        compiler_params=params(60),
        name="forward",
    )(cells, *ring, obs_bias[None], *fetched)

    side = jax.ShapeDtypeStruct((rows, 2, depth), BF)
    edge = jax.ShapeDtypeStruct((2, width, depth), BF)
    dforecast, head, tail, left, right = pl.pallas_call(
        scatter_kernel,
        out_shape=(jax.ShapeDtypeStruct((rows, width, depth), F32), edge, edge, side, side),
        in_specs=[VMEM] * 3 + [HBM] * 3,
        out_specs=(VMEM,) * 5,
        scratch_shapes=[
            pltpu.VMEM((taken, channels), F32),
            pltpu.VMEM((taken, hidden_units), BF),
            pltpu.SemaphoreType.DMA((taken // GROUP, 2)),
            pltpu.SMEM((taken,), jnp.int32),
            pltpu.SemaphoreType.DMA(()),
            pltpu.VMEM((taken, depth), F32),
        ]
        + [pltpu.VMEM((rows * width + 8, depth), F32)] * TOTALS,
        compiler_params=params(45),
        name="scatter",
    )(obs_out.T, obs_in.T, radiance, predicted, z_slope, cells)

    top, bottom = rows_around(head, tail)
    ring = (top, bottom, *columns_around(top, bottom, left, right)[0])
    return pl.pallas_call(
        backward_kernel,
        out_shape=jax.ShapeDtypeStruct((rows, width, depth), F32),
        in_specs=[VMEM] * 8,
        out_specs=HBM,
        scratch_shapes=conv_scratch(rows, width, depth)
        + [pltpu.VMEM((rows, width, depth), F32), pltpu.SemaphoreType.DMA((8,))],
        compiler_params=params(34),
        name="backward",
    )(dforecast, *ring, second_back, first_back, slope)


def solution(mesh):
    placed = (
        P("lat", "lon", None),
        P(),
        P(),
        P(),
        P(),
        P(),
        P(("lat", "lon"), None, None, None),
        P(("lat", "lon"), None),
        P(("lat", "lon"), None, None),
    )
    return jax.shard_map(
        per_device, mesh=mesh, in_specs=placed, out_specs=P("lat", "lon", None), check_vma=False
    )
```

```python
import jax
import jax.numpy as jnp
from jax import lax
from jax.experimental import pallas as pl
from jax.experimental.pallas import tpu as pltpu
from jax.sharding import PartitionSpec as P

BF = jnp.bfloat16
F32 = jnp.float32
WIDE = 128
PAD = 136
BLOCK = 512
GROUP = 1024
TOTALS = 4


def sigmoid(value):
    return 0.5 * jnp.tanh(0.5 * value) + 0.5


def pair_weights(kernel_ref, out_ref):
    depth = kernel_ref.shape[-1]
    zero = jnp.zeros((depth, depth), BF)
    for row in range(4):
        for col in range(3):
            at = (row * 3 + col) * depth
            out_ref[at : at + depth, :depth] = kernel_ref[row, col] if row < 3 else zero
            out_ref[at : at + depth, depth:] = kernel_ref[row - 1, col] if row > 0 else zero


def flipped_weights(kernel_ref, out_ref):
    depth = kernel_ref.shape[-1]
    zero = jnp.zeros((depth, depth), BF)
    for row in range(4):
        for col in range(3):
            at = (row * 3 + col) * depth
            out_ref[at : at + depth, :depth] = kernel_ref[2 - row, 2 - col].T if row < 3 else zero
            out_ref[at : at + depth, depth:] = kernel_ref[3 - row, 2 - col].T if row > 0 else zero


def clear_outside(ring):
    lat = lax.axis_index("lat")
    last = ring.shape[0] - 1
    ring[0, 0] = jnp.where(lat > 0, ring[0, 0], 0.0)
    ring[last, 1] = jnp.where(lat < lax.axis_size("lat") - 1, ring[last, 1], 0.0)


def taps_across(source_ref, taps_ref, start, width, first=0, last=None):
    depth = source_ref.shape[-1]
    of = slice(first, source_ref.shape[0] if last is None else last)
    for col in range(3):
        taps_ref[of, :, :, col * depth : (col + 1) * depth] = source_ref[
            of, :, start + col : start + col + width, :
        ].astype(BF)


def row_pairs(taps_ref, weights_ref, first, last):
    count, width, wide = last - first, taps_ref.shape[2], taps_ref.shape[3]
    rows = [
        taps_ref[first + a // 2 : last + a // 2, a % 2].reshape(count * width, wide)
        for a in range(4)
    ]
    total = jnp.dot(
        jnp.concatenate(rows, axis=1), weights_ref[...], preferred_element_type=F32
    )
    depth = wide // 3
    return (
        total[:, :depth].reshape(count, width, depth),
        total[:, depth:].reshape(count, width, depth),
    )


def spans(total, pieces):
    cuts = [total * i // pieces for i in range(pieces + 1)]
    return list(zip(cuts[:-1], cuts[1:]))


def pad_rim(padded_ref, top_ref, bottom_ref, left_ref, right_ref):
    pairs = padded_ref.shape[0]
    width = top_ref.shape[1]
    padded_ref[0, :, 6 : 6 + width, :] = top_ref[...].astype(F32)
    padded_ref[pairs - 1, :, 6 : 6 + width, :] = bottom_ref[...].astype(F32)
    sides = (pairs - 2, 2, 2, padded_ref.shape[-1])
    padded_ref[1 : pairs - 1, :, 6:8, :] = left_ref[...].astype(F32).reshape(sides)
    padded_ref[1 : pairs - 1, :, 4 + width : 6 + width, :] = right_ref[...].astype(F32).reshape(
        sides
    )


def forward_kernel(
    cells_ref, top_ref, bottom_ref, left_ref, right_ref, bias_ref,
    x_hbm, first_hbm, second_hbm, into_hbm, out_hbm,
    predicted_hbm, z_slope_hbm, slope_hbm, second_back_hbm, first_back_hbm, cells_hbm,
    padded, taps_one, hidden, taps_two, weights_one, weights_two, forecast, state,
    x_ref, first_ref, second_ref, into_ref, out_ref, sems,
    predicted_ref, z_slope_ref, slope_ref, second_back_ref, first_back_ref, out_sems,
):
    leaving = []

    def leave(source, into):
        leaving.append(pltpu.make_async_copy(source, into, out_sems.at[len(leaving)]))
        leaving[-1].start()

    sources = (x_hbm, first_hbm, second_hbm, into_hbm, out_hbm)
    fetched = (x_ref, first_ref, second_ref, into_ref, out_ref)
    copies = [
        pltpu.make_async_copy(source, into, sems.at[k])
        for k, (source, into) in enumerate(zip(sources, fetched))
    ]
    for copy in copies:
        copy.start()
    rows, width, depth = x_ref.shape
    for copy in copies:
        copy.wait()
    pair_weights(first_ref, weights_one)
    pair_weights(second_ref, weights_two)
    padded[1 : rows // 2 + 1, :, 8 : 8 + width, :] = (
        x_ref[...].astype(F32).reshape(rows // 2, 2, width, depth)
    )
    pad_rim(padded, top_ref, bottom_ref, left_ref, right_ref)
    taps_across(padded, taps_one, 6, WIDE)
    pairs = rows // 2 + 1
    for first, last in spans(pairs, 3):
        for odd, pre in enumerate(row_pairs(taps_one, weights_one, first, last)):
            sig = sigmoid(pre)
            hidden[first:last, odd] = pre * sig
            slope_ref[first:last, odd] = sig * (1.0 + pre * (1.0 - sig))
    leave(slope_ref, slope_hbm)
    clear_outside(hidden)
    taps_across(hidden, taps_two, 0, width)
    for first, last in spans(rows // 2, 4):
        for odd, change in enumerate(row_pairs(taps_two, weights_two, first, last)):
            for pair in range(first, last):
                row = 2 * pair + odd
                forecast[row * width : (row + 1) * width] = (
                    (x_ref[row].astype(F32) + change[pair - first]).astype(BF).astype(F32)
                )
    forecast[rows * width :] = jnp.zeros((forecast.shape[0] - rows * width, depth), F32)
    flipped_weights(second_ref, second_back_ref)
    flipped_weights(first_ref, first_back_ref)
    leave(cells_ref, cells_hbm.at[pl.ds(0, cells_ref.shape[0])])
    leave(second_back_ref, second_back_hbm)
    leave(first_back_ref, first_back_hbm)

    def take(slot, carry):
        state[pl.ds(slot, 1), :] = forecast[pl.ds(cells_ref[slot], 1), :]
        return carry

    taken = state.shape[0]
    lax.fori_loop(0, taken, take, 0, unroll=64)
    for first in range(0, taken, BLOCK):
        at = slice(first, first + BLOCK)
        z = jnp.dot(state[at].astype(BF), into_ref[...], preferred_element_type=F32)
        z = z + bias_ref[...]
        sig = sigmoid(z)
        z_slope_ref[at] = (sig * (1.0 + z * (1.0 - sig))).astype(BF)
        predicted_ref[at] = jnp.dot(
            (z * sig).astype(BF), out_ref[...], preferred_element_type=F32
        )
        leave(predicted_ref.at[at], predicted_hbm.at[at])
        leave(z_slope_ref.at[at], z_slope_hbm.at[at])
    for copy in leaving:
        copy.wait()


def scatter_kernel(
    out_t_ref, into_t_ref, radiance_ref, predicted_hbm, z_slope_hbm, cells_hbm,
    total_ref, head_ref, tail_ref, left_ref, right_ref,
    predicted, z_slope, sems, cells_ref, cells_sem, grads, *parts,
):
    taken = grads.shape[0]
    cells_copy = pltpu.make_async_copy(cells_hbm.at[pl.ds(0, taken)], cells_ref, cells_sem)
    cells_copy.start()
    blocks = [slice(first, first + GROUP) for first in range(0, taken, GROUP)]
    copies = [
        [
            pltpu.make_async_copy(source.at[at], into.at[at], sems.at[k, j])
            for j, (source, into) in enumerate(
                ((predicted_hbm, predicted), (z_slope_hbm, z_slope))
            )
        ]
        for k, at in enumerate(blocks)
    ]
    for group in copies:
        for copy in group:
            copy.start()
    for part in parts:
        part[...] = jnp.zeros(part.shape, F32)
    cells_copy.wait()

    def add(group, carry):
        slots = [group * len(parts) + k for k in range(len(parts))]
        ats = [pl.ds(cells_ref[slot], 1) for slot in slots]
        sums = [
            part[at, :] + grads[pl.ds(slot, 1), :] for part, at, slot in zip(parts, ats, slots)
        ]
        for part, at, value in zip(parts, ats, sums):
            part[at, :] = value
        return carry

    for at, group in zip(blocks, copies):
        for copy in group:
            copy.wait()
        misfit = (predicted[at] - radiance_ref[at].astype(F32)).astype(BF)
        back = jnp.dot(misfit, out_t_ref[...], preferred_element_type=F32)
        grads[at] = jnp.dot(
            (back * z_slope[at].astype(F32)).astype(BF),
            into_t_ref[...],
            preferred_element_type=F32,
        )
        lax.fori_loop(at.start // len(parts), at.stop // len(parts), add, 0, unroll=8)
    rows, width, depth = total_ref.shape
    total = parts[0][: rows * width]
    for part in parts[1:]:
        total = total + part[: rows * width]
    total = total.reshape(rows, width, depth)
    total_ref[...] = total
    head_ref[...] = total[:2].astype(BF)
    tail_ref[...] = total[rows - 2 :].astype(BF)
    left_ref[...] = total_ref[:, 0:2, :].astype(BF)
    right_ref[...] = total_ref[:, width - 2 : width, :].astype(BF)


def backward_kernel(
    d_ref, top_ref, bottom_ref, left_ref, right_ref, weights_one, weights_two, slope_ref,
    out_hbm,
    padded, taps_one, change, taps_two, out, sems,
):
    rows, width, depth = out.shape
    pairs = rows // 2 + 1
    pad_rim(padded, top_ref, bottom_ref, left_ref, right_ref)
    made = 0
    for first, last in spans(pairs, 6):
        low, high = max(made, 1), min(last + 1, pairs)
        padded[low:high, :, 8 : 8 + width] = d_ref[2 * low - 2 : 2 * high - 2].reshape(
            high - low, 2, width, depth
        )
        taps_across(padded, taps_one, 6, WIDE, made, last + 1)
        made = last + 1
        for odd, dhidden in enumerate(row_pairs(taps_one, weights_one, first, last)):
            change[first:last, odd] = dhidden * slope_ref[first:last, odd]
    clear_outside(change)
    made = 0
    leaving = []
    for k, (first, last) in enumerate(spans(rows // 2, 8)):
        taps_across(change, taps_two, 0, width, made, last + 1)
        made = last + 1
        for odd, back in enumerate(row_pairs(taps_two, weights_two, first, last)):
            for pair in range(first, last):
                out[2 * pair + odd] = d_ref[2 * pair + odd] + back[pair - first]
        at = slice(2 * first, 2 * last)
        leaving.append(pltpu.make_async_copy(out.at[at], out_hbm.at[at], sems.at[k]))
        leaving[-1].start()
    for copy in leaving:
        copy.wait()


VMEM = pl.BlockSpec(memory_space=pltpu.VMEM)
SMEM = pl.BlockSpec(memory_space=pltpu.SMEM)
HBM = pl.BlockSpec(memory_space=pltpu.HBM)


def params(mebibytes):
    return pltpu.CompilerParams(vmem_limit_bytes=mebibytes * 1024 * 1024)


def conv_scratch(rows, width, depth):
    return [
        pltpu.VMEM((rows // 2 + 2, 2, PAD, depth), F32),
        pltpu.VMEM((rows // 2 + 2, 2, WIDE, 3 * depth), BF),
        pltpu.VMEM((rows // 2 + 1, 2, WIDE, depth), F32),
        pltpu.VMEM((rows // 2 + 1, 2, width, 3 * depth), BF),
    ]


def swapped(array, axis, first, around):
    count = lax.axis_size(axis)
    pairs = [(i, (i + 1) % count) for i in range(first, count, 2) if around or i + 1 < count]
    return lax.ppermute(array, axis, [way for i, j in pairs for way in ((i, j), (j, i))])


def neighbours(low, high, axis, around, after=()):
    even = lax.rem(lax.axis_index(axis), 2) == 0
    one = swapped(jnp.where(even, high, low), axis, 0, around)
    two = swapped(jnp.where(even, low, high), axis, 1, around)
    two, after = lax.optimization_barrier((two, after))
    return (jnp.where(even, two, one), jnp.where(even, one, two)), after


def ring_around(head, tail, left, right, beside=(), after=()):
    (left, right), _ = neighbours(left, right, "lon", True)
    left, right, beside = lax.optimization_barrier((left, right, beside))
    head = jnp.concatenate([left[:2], head, right[:2]], axis=1)
    tail = jnp.concatenate([left[-2:], tail, right[-2:]], axis=1)
    (top, bottom), after = neighbours(head, tail, "lat", False, after)
    return (top, bottom, left, right), beside, after


def per_device(
    starting_vector, conv_first, later_stencil_matrix, obs_in, obs_bias, obs_out,
    innovations, counts, columns,
):
    rows, width, depth = starting_vector.shape
    lon_count, slots, channels = innovations.shape[1:]
    hidden_units = obs_in.shape[1]
    taken = lon_count * slots
    pairs = rows // 2 + 1

    live = lax.iota(jnp.int32, slots)[None, :] < counts[0][:, None]
    cells = jnp.where(live, columns[0], rows * width)
    cells = lax.all_to_all(cells, "lon", 0, 0, tiled=True).reshape(-1)
    x = starting_vector
    ring, cells, radiance = ring_around(
        x[:2], x[-2:], x[:, :2], x[:, -2:], cells, innovations[0]
    )
    radiance = lax.all_to_all(radiance, "lon", 0, 0, tiled=True).reshape(taken, channels)

    weights = jax.ShapeDtypeStruct((12 * depth, 2 * depth), BF)
    fetched = (x, conv_first, later_stencil_matrix, obs_in, obs_out)
    predicted, z_slope, slope, second_back, first_back, cells = pl.pallas_call(
        forward_kernel,
        out_shape=(
            jax.ShapeDtypeStruct((taken, channels), F32),
            jax.ShapeDtypeStruct((taken, hidden_units), BF),
            jax.ShapeDtypeStruct((pairs, 2, WIDE, depth), F32),
            weights,
            weights,
            jax.ShapeDtypeStruct((taken * 1024,), jnp.int32),
        ),
        in_specs=[SMEM] + [VMEM] * 5 + [HBM] * 5,
        out_specs=(HBM,) * 6,
        scratch_shapes=conv_scratch(rows, width, depth)
        + [pltpu.VMEM((12 * depth, 2 * depth), BF)] * 2
        + [pltpu.VMEM((rows * width + 8, depth), F32), pltpu.VMEM((taken, depth), F32)]
        + [pltpu.VMEM(array.shape, array.dtype) for array in fetched]
        + [pltpu.SemaphoreType.DMA((len(fetched),))]
        + [
            pltpu.VMEM((taken, channels), F32),
            pltpu.VMEM((taken, hidden_units), BF),
            pltpu.VMEM((pairs, 2, WIDE, depth), F32),
            pltpu.VMEM(weights.shape, BF),
            pltpu.VMEM(weights.shape, BF),
            pltpu.SemaphoreType.DMA((4 + 2 * taken // BLOCK,)),
        ],
        compiler_params=params(60),
        name="forward",
    )(cells, *ring, obs_bias[None], *fetched)

    side = jax.ShapeDtypeStruct((rows, 2, depth), BF)
    edge = jax.ShapeDtypeStruct((2, width, depth), BF)
    dforecast, head, tail, left, right = pl.pallas_call(
        scatter_kernel,
        out_shape=(jax.ShapeDtypeStruct((rows, width, depth), F32), edge, edge, side, side),
        in_specs=[VMEM] * 3 + [HBM] * 3,
        out_specs=(VMEM,) * 5,
        scratch_shapes=[
            pltpu.VMEM((taken, channels), F32),
            pltpu.VMEM((taken, hidden_units), BF),
            pltpu.SemaphoreType.DMA((taken // GROUP, 2)),
            pltpu.SMEM((taken,), jnp.int32),
            pltpu.SemaphoreType.DMA(()),
            pltpu.VMEM((taken, depth), F32),
        ]
        + [pltpu.VMEM((rows * width + 8, depth), F32)] * TOTALS,
        compiler_params=params(45),
        name="scatter",
    )(obs_out.T, obs_in.T, radiance, predicted, z_slope, cells)

    ring, _, _ = ring_around(head, tail, left, right)
    return pl.pallas_call(
        backward_kernel,
        out_shape=jax.ShapeDtypeStruct((rows, width, depth), F32),
        in_specs=[VMEM] * 8,
        out_specs=HBM,
        scratch_shapes=conv_scratch(rows, width, depth)
        + [pltpu.VMEM((rows, width, depth), F32), pltpu.SemaphoreType.DMA((8,))],
        compiler_params=params(34),
        name="backward",
    )(dforecast, *ring, second_back, first_back, slope)


def solution(mesh):
    placed = (
        P("lat", "lon", None),
        P(),
        P(),
        P(),
        P(),
        P(),
        P(("lat", "lon"), None, None, None),
        P(("lat", "lon"), None),
        P(("lat", "lon"), None, None),
    )
    return jax.shard_map(
        per_device, mesh=mesh, in_specs=placed, out_specs=P("lat", "lon", None), check_vma=False
    )
```
